128 devices in a mesh: strip: 4 (over y), seq: 32 (over z, x, core).
Axes of the slice: x: 4, y: 4, z: 4, core: 2. Of those that a mesh axis runs over, the one named last changes fastest.
Arguments:
- features: bfloat16 [192, 32, 16, 128], P('seq', 'strip'), may hold values from -6 to 6
- conv_weight: bfloat16 [3, 3, 3, 128, 128], replicated, may hold values from -0.109375 to 0.109375
- latent_weight: bfloat16 [512, 128], replicated, may hold values from -0.25 to 0.25
- embed_weight: bfloat16 [128, 3072], replicated, may hold values from -0.5 to 0.5
- qkv_weight: bfloat16 [3072, 3, 3072], P(None, None, 'strip'), may hold values from -0.109375 to 0.109375
- modulation: bfloat16 [64, 2, 3072], replicated, may hold values from -16 to 16, as said below
- clip_frames: int32 [64], replicated, may hold values from 1 to 8, as said below
- clip_owner: int32 [64], replicated, may hold values from 0 to 31, as said below
- clip_offset: int32 [64], replicated, may hold values from 0 to 8, as said below
Outputs:
- attention_out: bfloat16 [32, 1152, 3072], P('seq', None, 'strip')
The draws below stay inside these ranges and needn't reach their ends.
Inputs may be any that keep to these rules, and one draw needn't show every extreme that they name: `clip_frames`: the clip frame counts sum to 192; every owner has exactly two clips, whose frames total at most 9; some owner has exactly 9 frames, in a clip of 1 frame and a clip of 8. `clip_owner`: every owner from 0 to 31 has exactly two clips. `clip_offset`: the two clips of an owner fill its frame slots from 0 on without gap or intersection, in either order. modulation[c, 0] is the shift and modulation[c, 1] the scale of clip c.
All inputs are finite; a program needn't handle non-finite values.
Results may differ from the reference program's by a relative error of at most 0.017.
The reference program's roundings to bfloat16 on the way count: a program that leaves them out, or rounds other values in their place, can miss the bound.
Values may be sent and summed in bfloat16 or wider, within the bound.
A program may use at most 128 MiB of HBM per device.

```python
import jax
import jax.numpy as jnp
from jax import lax

C = 128
LAT = 128
D = 3072
HEAD = 128
F_DEV = 6
WP = 16
HTF = 16
FRAMES = 192
CAPF = 9
NCLIP = 64


def packing(key):
    owners = NCLIP // 2
    half = owners // 2
    spread = F_DEV // 2
    key_extra, key_order, key_first, key_values = jax.random.split(key, 4)
    extra = jax.random.randint(key_extra, (half,), 0, spread + 1)
    extra = extra.at[0].set(spread)
    order = jax.random.permutation(key_order, owners)
    pair_load = jnp.concatenate([F_DEV + extra, F_DEV - extra]).astype(jnp.int32)
    load = jnp.zeros((owners,), jnp.int32).at[order].set(pair_load)
    first = jax.random.randint(key_first, (owners,), 1, load).astype(jnp.int32)
    first = first.at[order[0]].set(F_DEV + spread - 1)
    value_frames = jnp.stack([first, load - first], axis=1).reshape(-1)
    value_offset = jnp.stack([jnp.zeros_like(first), first], axis=1).reshape(-1)
    clip_value = jax.random.permutation(key_values, NCLIP).astype(jnp.int32)
    return (value_frames[clip_value], clip_value // 2, value_offset[clip_value])


def draw_clip_frames(key, part):
    return packing(key)[0]


def draw_clip_owner(key, part):
    return packing(key)[1]


def draw_clip_offset(key, part):
    return packing(key)[2]


def draw_modulation(key, part):
    key = jax.random.fold_in(key, 11)
    key_base = jax.random.fold_in(key, 0)
    return jnp.clip(jax.random.normal(key_base, (NCLIP, 2, D), jnp.float32) * 0.5, -4.0, 4.0).astype(jnp.bfloat16)


def steps_of(rng, shape, shards, least, high):
    def one(position, parts):
        draws = jax.random.uniform(jax.random.fold_in(jax.random.fold_in(rng, 6), position), (parts,), jnp.float32, least / len(shards), high / len(shards))
        return jnp.repeat(jnp.exp(draws), shape[position] // parts).reshape((-1,) + (1,) * (len(shape) - position - 1))

    loudness = one(*shards[0])
    for cut in shards[1:]:
        loudness = loudness * one(*cut)
    return loudness


def normal_values(stream_key, extent, scale, reach, pieces=(), kind=jnp.bfloat16):
    result = jax.random.normal(stream_key, extent, jnp.float32) * scale
    if len(pieces) > 0:
        result = steps_of(stream_key, extent, pieces, -0.22, 0.18) * result
    return jnp.clip(result, min=-reach, max=reach).astype(kind)


def setup_inputs(seed: int = 0) -> dict:
    key_list = jax.random.split(jax.random.key(seed), 10)
    features = normal_values(key_list[0], (FRAMES, 2 * HTF, WP, C), 1.0, 6.0, ((0, 32), (1, 4)))
    conv_weight = normal_values(key_list[1], (3, 3, 3, C, C), (27 * C) ** -0.5, 0.109375)
    latent_weight = normal_values(key_list[2], (4 * C, LAT), (4 * C) ** -0.5, 0.25)
    embed_weight = normal_values(key_list[3], (LAT, D), LAT ** -0.5, 0.5)
    qkv_weight = normal_values(key_list[4], (D, 3, D), D ** -0.5, 0.109375, ((2, 4),))
    modulation = draw_modulation(jax.random.fold_in(key_list[9], 71), 0)
    clip_frames = draw_clip_frames(jax.random.fold_in(key_list[9], 71), 0)
    clip_owner = draw_clip_owner(jax.random.fold_in(key_list[9], 71), 0)
    clip_offset = draw_clip_offset(jax.random.fold_in(key_list[9], 71), 0)
    return {"features": features, "conv_weight": conv_weight, "latent_weight": latent_weight, "embed_weight": embed_weight, "qkv_weight": qkv_weight, "modulation": modulation, "clip_frames": clip_frames, "clip_owner": clip_owner, "clip_offset": clip_offset}


EPSILON = 1e-06

def frame_clip(numbers, starts):
    return lax.optimization_barrier(jnp.sum((numbers[:, None] >= starts[None, :]).astype(jnp.int32), axis=1)) - 1

def reference(features, conv_weight, latent_weight, embed_weight, qkv_weight, modulation, clip_frames, clip_owner, clip_offset):
    frames_all, rows, columns, channels = features.shape
    starts = jnp.cumsum(clip_frames) - clip_frames
    numbers = jnp.arange(frames_all, dtype=jnp.int32)
    clip_ids = frame_clip(numbers, starts)
    padded_ids = jnp.concatenate([jnp.full((2,), -1, jnp.int32), clip_ids])
    framed = jnp.pad(features, ((2, 0), (1, 1), (1, 1), (0, 0)))
    hidden = jnp.zeros((frames_all, rows, columns, conv_weight.shape[4]), jnp.float32)
    for back in range(3):
        source = framed[2 - back:2 - back + frames_all]
        keep = padded_ids[2 - back:2 - back + frames_all] == clip_ids
        source = jnp.where(keep[:, None, None, None], source, jnp.zeros_like(source)).astype(jnp.float32)
        for down in range(3):
            for across in range(3):
                window = source[:, down:down + rows, across:across + columns]
                hidden = hidden + jnp.einsum('fhwi,io->fhwo', window, conv_weight[back, down, across].astype(jnp.float32))
    active = jax.nn.silu(hidden).astype(jnp.bfloat16)
    token_rows = rows // 2
    token_cols = columns // 2
    patches = active.reshape(frames_all, token_rows, 2, token_cols, 2, channels).transpose(0, 1, 3, 2, 4, 5)
    patches = patches.reshape(frames_all * token_rows * token_cols, 4 * channels)
    latent = jnp.dot(patches, latent_weight, preferred_element_type=jnp.float32).astype(jnp.bfloat16)
    latent = latent.reshape(frames_all, token_rows, token_cols, latent_weight.shape[1])
    target_owner = clip_owner[clip_ids]
    target_slot = clip_offset[clip_ids] + numbers - starts[clip_ids]
    owners = NCLIP // 2
    packed = jnp.zeros((owners, CAPF) + latent.shape[1:], jnp.bfloat16).at[target_owner, target_slot].set(latent)
    slot_numbers = jnp.arange(CAPF, dtype=jnp.int32)
    owner_numbers = jnp.arange(owners, dtype=jnp.int32)
    match = (clip_owner[None, None, :] == owner_numbers[:, None, None]) & (slot_numbers[None, :, None] >= clip_offset[None, None, :]) & (slot_numbers[None, :, None] < (clip_offset + clip_frames)[None, None, :])
    match_int = match.astype(jnp.int32)
    clip_numbers = jnp.arange(NCLIP, dtype=jnp.int32)
    slot_clip = lax.optimization_barrier(jnp.sum(match_int * clip_numbers[None, None, :], axis=2)) + lax.optimization_barrier(jnp.sum(match_int, axis=2)) - 1
    shift_scale = jnp.einsum('osc,cpd->ospd', match.astype(jnp.float32), modulation.astype(jnp.float32), precision=lax.Precision.HIGHEST)
    per_frame = token_rows * token_cols

    def one_owner(inputs):
        owner_packed, owner_clip, owner_mod = inputs
        tokens = owner_packed.reshape(-1, owner_packed.shape[-1])
        base = jnp.dot(tokens, embed_weight, preferred_element_type=jnp.float32)
        mean = lax.optimization_barrier(jnp.mean(base, axis=1, keepdims=True))
        centered = base - mean
        variance = lax.optimization_barrier(jnp.mean(centered * centered, axis=1, keepdims=True))
        normal = (centered * lax.rsqrt(variance + EPSILON)).reshape(CAPF, per_frame, -1)
        mixed = normal * (1.0 + owner_mod[:, 1][:, None, :]) + owner_mod[:, 0][:, None, :]
        mixed = mixed.astype(jnp.bfloat16).reshape(CAPF * per_frame, -1)
        width = mixed.shape[1]
        projected = jnp.dot(mixed, qkv_weight.reshape(width, 3 * width), preferred_element_type=jnp.float32)
        projected = lax.optimization_barrier(projected.astype(jnp.bfloat16)).astype(jnp.float32)
        projected = projected.reshape(CAPF * per_frame, 3, width // HEAD, HEAD)
        token_clip = jnp.repeat(owner_clip, per_frame)
        allowed = token_clip[:, None] == token_clip[None, :]
        scores = jnp.einsum('qhd,khd->hqk', projected[:, 0], projected[:, 1]) * HEAD ** (-0.5)
        scores = jnp.where(allowed[None], scores, -1e+30)
        top = lax.optimization_barrier(jnp.max(scores, axis=2, keepdims=True))
        raised = jnp.exp(scores - top)
        weights = raised / lax.optimization_barrier(jnp.sum(raised, axis=2, keepdims=True))
        weights = lax.optimization_barrier(weights.astype(jnp.bfloat16)).astype(jnp.float32)
        attended = jnp.einsum('hqk,khd->qhd', weights, projected[:, 2])
        return attended.reshape(CAPF * per_frame, width).astype(jnp.bfloat16)
    return lax.map(one_owner, (packed, slot_clip, shift_scale))
```

```python
import functools
import jax
import jax.numpy as jnp
from jax import lax
from jax.experimental import pallas as pl
from jax.experimental.pallas import tpu as pltpu
from jax.sharding import PartitionSpec as P

HEAD = 128


EPSILON = 1e-06


EPS = 1e-6
CAP = 9
PF = 128
D = 3072
C2 = 128**-0.5 * 1.4426950408889634

def attn_block(q, k, v1):
    s = lax.dot_general(q, k, (((1,), (1,)), ((), ())), preferred_element_type=jnp.float32)
    m = jnp.max(s, axis=1, keepdims=True)
    e = jnp.exp2((s - m) * C2).astype(jnp.bfloat16)
    o = jnp.dot(e, v1, preferred_element_type=jnp.float32)
    return (o[:, :HEAD] * (1.0 / o[:, HEAD:])).astype(jnp.bfloat16)

def kernel(seg_ref, tok_ref, whl_ref, g_ref, mod_ref, w_ref, o_ref, mod_s, q_s, k_s, v_s, *, sparse):
    p = pl.program_id(0)
    @pl.when(p == 0)
    def _():
        v_s[...] = jnp.ones_like(v_s)
        def slot(s, _):
            rows = pl.ds(pl.multiple_of(s*PF, PF), PF)
            t = tok_ref[rows, :]
            tt = jnp.concatenate([t, t], axis=1)
            tg = jnp.dot(tt, g_ref[...], preferred_element_type=jnp.float32)
            var = jnp.sum(tg * t.astype(jnp.float32), axis=1, keepdims=True) * (1.0/D)
            rstd = lax.rsqrt(jnp.maximum(var, 0.0) + EPS)
            c = seg_ref[s]
            valid = (c >= 0).astype(jnp.float32)
            ms = mod_ref[jnp.maximum(c, 0)].astype(jnp.float32) * valid
            NB = 512
            for n in range(0, D, NB):
                x = jnp.dot(tt, whl_ref[:, n:n+NB], preferred_element_type=jnp.float32)
                x = (x * rstd) * (1.0 + ms[1:2, n:n+NB]) + ms[0:1, n:n+NB]
                mod_s[rows, n:n+NB] = x.astype(jnp.bfloat16)
            return 0
        lax.fori_loop(0, CAP, slot, 0)
    R = 384
    def rowblk(r, _):
        rows = pl.ds(pl.multiple_of(r*R, R), R)
        x = mod_s[rows, :]
        q_s[rows, :] = jnp.dot(x, w_ref[0], preferred_element_type=jnp.float32).astype(jnp.bfloat16)
        k_s[rows, :] = jnp.dot(x, w_ref[1], preferred_element_type=jnp.float32).astype(jnp.bfloat16)
        vv = jnp.dot(x, w_ref[2], preferred_element_type=jnp.float32).astype(jnp.bfloat16)
        v_s[rows, 0:128] = vv[:, :128]
        v_s[rows, 256:384] = vv[:, 128:]
        return 0
    lax.fori_loop(0, CAP*PF//R, rowblk, 0)
    def qf(i, _):
        rows = pl.ds(pl.multiple_of(i*PF, PF), PF)
        a = seg_ref[CAP+i]; n = seg_ref[2*CAP+i]
        def branch(nn):
            def go():
                kr = pl.ds(pl.multiple_of(a*PF, PF), nn*PF)
                for h in range(2):
                    hs = slice(h*HEAD, (h+1)*HEAD)
                    o_ref[rows, hs] = attn_block(q_s[rows, hs], k_s[kr, hs], v_s[kr, h*256:(h+1)*256])
            return go
        for nn in range(1, CAP+1):
            pl.when(n == nn)(branch(nn))
        return 0
    lax.fori_loop(0, CAP, qf, 0)

def call(seg, tokens, whl, ghl, mod, w3):
    T = CAP*PF
    return pl.pallas_call(
        functools.partial(kernel, sparse=True),
        grid_spec=pltpu.PrefetchScalarGridSpec(
            num_scalar_prefetch=1, grid=(3,),
            in_specs=[pl.BlockSpec((T,128), lambda p, s:(0,0)),
                      pl.BlockSpec((256,D), lambda p, s:(0,0)),
                      pl.BlockSpec((256,128), lambda p, s:(0,0)),
                      pl.BlockSpec((64,2,D), lambda p, s:(0,0,0)),
                      pl.BlockSpec((3,D,256), lambda p, s:(0,0,p))],
            out_specs=pl.BlockSpec((T,256), lambda p, s:(0,p)),
            scratch_shapes=[pltpu.VMEM((T,D),jnp.bfloat16), pltpu.VMEM((T,256),jnp.bfloat16),
                            pltpu.VMEM((T,256),jnp.bfloat16), pltpu.VMEM((T,512),jnp.bfloat16)]),
        out_shape=jax.ShapeDtypeStruct((T,768), jnp.bfloat16),
        compiler_params=pltpu.CompilerParams(vmem_limit_bytes=56*2**20),
        name="block",
    )(seg, tokens, whl, ghl, mod, w3)

def prep(embed):
    w = embed.astype(jnp.float32)
    wc = w - jnp.mean(w, axis=1, keepdims=True)
    hi = wc.astype(jnp.bfloat16); lo = (wc - hi.astype(jnp.float32)).astype(jnp.bfloat16)
    g = jnp.dot(wc, wc.T, precision=lax.Precision.HIGHEST)
    ghi = g.astype(jnp.bfloat16); glo = (g - ghi.astype(jnp.float32)).astype(jnp.bfloat16)
    return jnp.concatenate([hi, lo]), jnp.concatenate([ghi, glo])


def extended(cells, sides, width):
    for axis, dim in sides:
        count = lax.axis_size(axis)
        ends = count - 1
        head = lax.slice_in_dim(cells, 0, width, axis=dim)
        tail = lax.slice_in_dim(cells, cells.shape[dim] - width, cells.shape[dim], axis=dim)
        cells = jnp.concatenate(
            [
                lax.ppermute(tail, axis, [(i, (i + 1) % count) for i in range(ends)]),
                cells,
                lax.ppermute(head, axis, [((i + 1) % count, i) for i in range(ends)]),
            ],
            axis=dim,
        )
    return cells


def shifted(value, axis, steps):
    count = lax.axis_size(axis)
    initial, last = (max(0, -steps), min(count, count - steps))
    return lax.ppermute(value, axis, [(source, source + steps) for source in range(initial, last)])


def frame_clip(numbers, starts):
    return jnp.sum((numbers[:, None] >= starts[None, :]).astype(jnp.int32), axis=1) - 1


def select_rows(row_number, total_rows, piece):
    select = (jnp.arange(total_rows, dtype=jnp.int32)[:, None] == row_number[None, :]).astype(
        piece.dtype
    )
    return jnp.dot(select, piece, preferred_element_type=jnp.float32)


def shards(
    features,
    conv_weight,
    latent_weight,
    embed_weight,
    qkv_weight,
    modulation,
    clip_frames,
    clip_owner,
    clip_offset,
):
    frames_dev, rows, columns, channels = features.shape
    strips = lax.axis_size("strip")
    owners = lax.axis_size("seq")
    seq_index = lax.axis_index("seq")
    clip_count = clip_frames.shape[0]
    capacity = frames_dev + frames_dev // 2
    starts = jnp.cumsum(clip_frames) - clip_frames
    clip_numbers = jnp.arange(clip_count, dtype=jnp.int32)
    padded = extended(features, (("strip", 1),), 1)
    history = shifted(padded[frames_dev - 2 :], "seq", 1)
    framed = jnp.pad(jnp.concatenate([history, padded], axis=0), ((0, 0), (0, 0), (1, 1), (0, 0)))
    numbers = seq_index * frames_dev - 2 + jnp.arange(frames_dev + 2, dtype=jnp.int32)
    clip_ids = frame_clip(numbers, starts)
    windows = []
    for back in range(3):
        source = framed[2 - back : 2 - back + frames_dev]
        keep = clip_ids[2 - back : 2 - back + frames_dev] == clip_ids[2:]
        source = jnp.where(keep[:, None, None, None], source, jnp.zeros_like(source))
        for down in range(3):
            for across in range(3):
                windows.append(source[:, down : down + rows, across : across + columns])
    stacked = jnp.concatenate(windows, axis=3).reshape(frames_dev * rows * columns, 27 * channels)
    hidden = jnp.dot(
        stacked, conv_weight.reshape(27 * channels, -1), preferred_element_type=jnp.float32
    )
    active = jax.nn.silu(hidden).astype(jnp.bfloat16)
    token_rows = rows // 2
    token_cols = columns // 2
    patches = active.reshape(frames_dev, token_rows, 2, token_cols, 2, channels).transpose(
        0, 1, 3, 2, 4, 5
    )
    patches = patches.reshape(frames_dev * token_rows * token_cols, 4 * channels)
    latent = jnp.dot(patches, latent_weight, preferred_element_type=jnp.float32).astype(
        jnp.bfloat16
    )
    latent_dim = latent.shape[1]
    latent = latent.reshape(frames_dev, token_rows * token_cols * latent_dim)
    latent = latent.reshape(frames_dev * token_rows * token_cols, latent_dim)
    per_strip = token_rows * token_cols
    frames_all = owners * frames_dev
    slot_numbers = jnp.arange(capacity, dtype=jnp.int32)
    match = (
        (clip_owner[None, :] == seq_index)
        & (slot_numbers[:, None] >= clip_offset[None, :])
        & (slot_numbers[:, None] < (clip_offset + clip_frames)[None, :])
    )
    match_int = match.astype(jnp.int32)
    any_clip = jnp.sum(match_int, axis=1)
    slot_clip = jnp.sum(match_int * clip_numbers[None, :], axis=1) + any_clip - 1
    frame = jnp.sum(match_int * (starts - clip_offset)[None, :], axis=1) + slot_numbers
    seg_start = jnp.sum(match_int * clip_offset[None, :], axis=1)
    seg_len = jnp.sum(match_int * clip_frames[None, :], axis=1)
    used = jnp.sum(any_clip)
    seg_start = jnp.where(any_clip > 0, seg_start, used)
    seg_len = jnp.where(any_clip > 0, seg_len, capacity - used)
    seg = jnp.concatenate([slot_clip, seg_start, seg_len])
    piece = lax.all_gather(latent, "seq", axis=0, tiled=True).reshape(frames_all, per_strip, latent_dim)
    mine = jnp.where((any_clip > 0)[:, None, None], piece[jnp.where(any_clip > 0, frame, 0)], jnp.zeros((), piece.dtype))
    tokens = lax.all_gather(mine, "strip", axis=1, tiled=True).reshape(-1, latent_dim)
    whl, ghl = prep(embed_weight)
    out = call(seg, tokens, whl, ghl, modulation, qkv_weight.transpose(1, 0, 2))
    return out.reshape(1, capacity * per_strip * strips, -1)


def solution(mesh):
    placed = (
        P("seq", "strip", None, None),
        P(),
        P(),
        P(),
        P(None, None, "strip"),
        P(),
        P(),
        P(),
        P(),
    )
    return jax.shard_map(
        shards, mesh=mesh, in_specs=placed, out_specs=P("seq", None, "strip"), check_vma=False
    )
```

```python
import functools

import jax
import jax.numpy as jnp
from jax import lax
from jax.experimental import pallas as pl
from jax.experimental.pallas import tpu as pltpu
from jax.sharding import PartitionSpec as P

EPS = 1e-6
HEAD = 128
CAP = 9
PF = 128
D = 3072
C2 = 128**-0.5 * 1.4426950408889634

def attn_block(q, k, v1):
    s = lax.dot_general(q, k, (((1,), (1,)), ((), ())), preferred_element_type=jnp.float32)
    m = jnp.max(s, axis=1, keepdims=True)
    e = jnp.exp2((s - m) * C2).astype(jnp.bfloat16)
    o = jnp.dot(e, v1, preferred_element_type=jnp.float32)
    return (o[:, :HEAD] * (1.0 / o[:, HEAD:])).astype(jnp.bfloat16)

def kernel(seg_ref, tok_ref, whl_ref, g_ref, mod_ref, w_ref, o_ref, mod_s, q_s, k_s, v_s, *, sparse):
    p = pl.program_id(0)
    @pl.when(p == 0)
    def _():
        v_s[...] = jnp.ones_like(v_s)
        def slot(s, _):
            rows = pl.ds(pl.multiple_of(s*PF, PF), PF)
            t = tok_ref[rows, :]
            tt = jnp.concatenate([t, t], axis=1)
            ttt = jnp.concatenate([t, t, t], axis=1)
            tg = jnp.dot(ttt, g_ref[...], preferred_element_type=jnp.float32)
            var = jnp.sum(tg * t.astype(jnp.float32), axis=1, keepdims=True) * (1.0/D)
            rstd = lax.rsqrt(jnp.maximum(var, 0.0) + EPS)
            c = seg_ref[s]
            valid = (c >= 0).astype(jnp.float32)
            ms = mod_ref[jnp.maximum(c, 0)].astype(jnp.float32) * valid
            NB = 512
            for n in range(0, D, NB):
                x = jnp.dot(tt, whl_ref[:, n:n+NB], preferred_element_type=jnp.float32)
                x = (x * rstd) * (1.0 + ms[1:2, n:n+NB]) + ms[0:1, n:n+NB]
                mod_s[rows, n:n+NB] = x.astype(jnp.bfloat16)
            return 0
        lax.fori_loop(0, CAP, slot, 0)
    R = 384
    def rowblk(r, _):
        rows = pl.ds(pl.multiple_of(r*R, R), R)
        x = mod_s[rows, :]
        q_s[rows, :] = jnp.dot(x, w_ref[0], preferred_element_type=jnp.float32).astype(jnp.bfloat16)
        k_s[rows, :] = jnp.dot(x, w_ref[1], preferred_element_type=jnp.float32).astype(jnp.bfloat16)
        vv = jnp.dot(x, w_ref[2], preferred_element_type=jnp.float32).astype(jnp.bfloat16)
        v_s[rows, 0:128] = vv[:, :128]
        v_s[rows, 256:384] = vv[:, 128:]
        return 0
    lax.fori_loop(0, CAP*PF//R, rowblk, 0)
    def qf(i, _):
        rows = pl.ds(pl.multiple_of(i*PF, PF), PF)
        a = seg_ref[CAP+i]; n = seg_ref[2*CAP+i]
        def branch(nn):
            def go():
                kr = pl.ds(pl.multiple_of(a*PF, PF), nn*PF)
                for h in range(2):
                    hs = slice(h*HEAD, (h+1)*HEAD)
                    o_ref[rows, hs] = attn_block(q_s[rows, hs], k_s[kr, hs], v_s[kr, h*256:(h+1)*256])
            return go
        for nn in range(1, CAP+1):
            pl.when(n == nn)(branch(nn))
        return 0
    lax.fori_loop(0, CAP, qf, 0)

def call(seg, tokens, whl, ghl, mod, w3):
    T = CAP*PF
    return pl.pallas_call(
        functools.partial(kernel, sparse=True),
        grid_spec=pltpu.PrefetchScalarGridSpec(
            num_scalar_prefetch=1, grid=(3,),
            in_specs=[pl.BlockSpec((T,128), lambda p, s:(0,0)),
                      pl.BlockSpec((256,D), lambda p, s:(0,0)),
                      pl.BlockSpec((384,128), lambda p, s:(0,0)),
                      pl.BlockSpec((64,2,D), lambda p, s:(0,0,0)),
                      pl.BlockSpec((3,D,256), lambda p, s:(0,0,p))],
            out_specs=pl.BlockSpec((T,256), lambda p, s:(0,p)),
            scratch_shapes=[pltpu.VMEM((T,D),jnp.bfloat16), pltpu.VMEM((T,256),jnp.bfloat16),
                            pltpu.VMEM((T,256),jnp.bfloat16), pltpu.VMEM((T,512),jnp.bfloat16)]),
        out_shape=jax.ShapeDtypeStruct((T,768), jnp.bfloat16),
        compiler_params=pltpu.CompilerParams(vmem_limit_bytes=56*2**20),
        name="block",
    )(seg, tokens, whl, ghl, mod, w3)


MESH = pl.DeviceIdType.MESH


def front_kernel(
    frames_ref, owner_ref, offset_ref, feat_ref, conv_ref, lat_ref, embed_ref,
    seg_ref, tok_ref, whl_ref, g_ref,
    F, X3, Wv, Lv, Ev, P, A, GA, GB, SEL, PART, T4, whl_s, kflag,
    lsem, hsend, hrecv, asend, arecv, bsend, brecv, csend, crecv, tsend, trecv,
):
    strip = lax.axis_index("strip")
    seq = lax.axis_index("seq")
    core = lax.rem(seq, 2)
    chip = seq // 2
    xx = lax.rem(chip, 4)
    zz = chip // 4
    up, down = lax.rem(strip + 3, 4), lax.rem(strip + 1, 4)
    prev, nxt = lax.rem(seq + 31, 32), lax.rem(seq + 1, 32)

    def at_x(d):
        return (zz * 4 + lax.rem(xx + d, 4)) * 2 + core

    def at_z(d):
        return (lax.rem(zz + d, 4) * 4 + xx) * 2 + core

    partner = chip * 2 + 1 - core

    loc = [
        pltpu.make_async_copy(feat_ref, F.at[2:8, 1:9], lsem.at[0]),
        pltpu.make_async_copy(conv_ref, Wv, lsem.at[1]),
        pltpu.make_async_copy(lat_ref, Lv, lsem.at[2]),
        pltpu.make_async_copy(embed_ref, Ev, lsem.at[3]),
    ]
    for c in loc:
        c.start()

    barrier = pltpu.get_barrier_semaphore()

    def hello(s, j):
        pl.semaphore_signal(barrier, inc=1, device_id=(s, j), device_id_type=MESH)

    for d in (1, 2, 3):
        hello(strip, at_x(d))
        hello(strip, at_z(d))
        hello(lax.rem(strip + d, 4), seq)
    hello(strip, partner)
    hello(up, prev)
    hello(down, prev)

    @pl.when(core == 0)
    def _():
        hello(strip, prev)

    base = seq * 6
    own = (seq, partner)
    zero = jnp.int32(0)

    def clip(c, carry):
        start, flags, acc = carry
        n, o, off = frames_ref[c], owner_ref[c], offset_ref[c]
        flags = tuple(jnp.where(start == base - 1 + i, 1, flags[i]) for i in range(7))
        out = []
        for w in range(2):
            sa, na, ca, db, nb, cb = acc[w]
            is_a = (o == own[w]) & (off == 0)
            is_b = (o == own[w]) & (off > 0)
            out.append((
                jnp.where(is_a, start, sa), jnp.where(is_a, n, na), jnp.where(is_a, c, ca),
                jnp.where(is_b, start - off, db), jnp.where(is_b, n, nb), jnp.where(is_b, c, cb),
            ))
        return start + n, flags, tuple(out)

    _, flags, acc = lax.fori_loop(
        0, 64, clip, (zero, (zero,) * 7, ((zero,) * 6,) * 2), unroll=4
    )
    sa, na, ca, db, nb, cb = acc[0]
    for s in range(9):
        in_a = s < na
        in_b = (s >= na) & (s < na + nb)
        seg_ref[s] = jnp.where(in_a, ca, jnp.where(in_b, cb, -1))
        seg_ref[9 + s] = jnp.where(in_a, 0, jnp.where(in_b, na, na + nb))
        seg_ref[18 + s] = jnp.where(in_a, na, jnp.where(in_b, nb, 9 - na - nb))

    loc[0].wait()
    pl.semaphore_wait(barrier, 12 + core)

    halo = []

    def send(src, dst, s, j):
        i = len(halo)
        c = pltpu.make_async_remote_copy(
            src_ref=src, dst_ref=dst, send_sem=hsend.at[i], recv_sem=hrecv.at[i],
            device_id=(s, j), device_id_type=MESH,
        )
        c.start()
        halo.append(c)

    send(F.at[6:8, 1:9], F.at[0:2, 1:9], strip, nxt)
    send(F.at[2:8, 8], F.at[2:8, 0], down, seq)
    send(F.at[2:8, 1], F.at[2:8, 9], up, seq)
    send(F.at[6:8, 8], F.at[0:2, 0], down, nxt)
    send(F.at[6:8, 1], F.at[0:2, 9], up, nxt)
    for c in halo:
        c.wait()

    @pl.when(strip == 0)
    def _():
        F[:, 0] = jnp.zeros_like(F[:, 0])

    @pl.when(strip == 3)
    def _():
        F[:, 9] = jnp.zeros_like(F[:, 9])

    def widen(g, _):
        x = F[g].reshape(160, 128).astype(jnp.float32)
        col = lax.rem(lax.broadcasted_iota(jnp.int32, (160, 128), 0), 16)
        left = jnp.where(col == 0, 0.0, pltpu.roll(x, 1, 0))
        right = jnp.where(col == 15, 0.0, pltpu.roll(x, 159, 0))
        X3[g, :, :, 0:128] = left.astype(jnp.bfloat16).reshape(10, 16, 128)
        X3[g, :, :, 128:256] = F[g]
        X3[g, :, :, 256:384] = right.astype(jnp.bfloat16).reshape(10, 16, 128)
        return 0

    lax.fori_loop(0, 8, widen, 0)
    loc[1].wait()
    rhs = jnp.concatenate([Wv[0], Wv[1], Wv[2]], axis=1)

    def taps(g, _):
        lhs = jnp.concatenate(
            [X3[g, d : d + 8].reshape(128, 384) for d in range(3)], axis=1
        )
        P[g] = jnp.dot(lhs, rhs, preferred_element_type=jnp.float32)
        return 0

    lax.fori_loop(0, 8, taps, 0)
    for f in range(6):
        not_start = 1 - flags[f + 1]
        k1 = not_start.astype(jnp.float32)
        k2 = (not_start * (1 - flags[f])).astype(jnp.float32)
        h = P[f + 2, :, 0:128] + k1 * P[f + 1, :, 128:256] + k2 * P[f, :, 256:384]
        a = h / (1.0 + jnp.exp(-h))
        A[f] = a.astype(jnp.bfloat16).astype(jnp.float32)
    loc[2].wait()
    for f in range(6):
        even = A[f, pl.ds(0, 64, stride=2)].reshape(4, 2, 8, 128)
        odd = A[f, pl.ds(1, 64, stride=2)].reshape(4, 2, 8, 128)
        patch = jnp.concatenate(
            [v[:, a].reshape(32, 128) for a in range(2) for v in (even, odd)], axis=1
        ).astype(jnp.bfloat16)
        lat = jnp.dot(patch, Lv[...], preferred_element_type=jnp.float32).astype(jnp.bfloat16)
        if f < 3:
            GA[zz, xx, f] = lat
        else:
            GB[xx, zz, f - 3] = lat

    def push(src, dst, ss, rs, j):
        return pltpu.make_async_remote_copy(
            src_ref=src, dst_ref=dst, send_sem=ss, recv_sem=rs,
            device_id=(strip, j), device_id_type=MESH,
        )

    first = []
    for i, d in enumerate((1, 3, 2)):
        first.append((
            push(GA.at[zz, xx], GA.at[zz, xx], asend.at[i], arecv.at[i], at_x(d)),
            push(GB.at[xx, zz], GB.at[xx, zz], asend.at[3 + i], arecv.at[3 + i], at_z(d)),
        ))
        for c in first[-1]:
            c.start()

    loc[3].wait()
    w = Ev[...].astype(jnp.float32)
    wc = w - jnp.mean(w, axis=1, keepdims=True)
    hi = wc.astype(jnp.bfloat16)
    lo = (wc - hi.astype(jnp.float32)).astype(jnp.bfloat16)
    whl_s[0:128] = hi
    whl_s[128:256] = lo
    whl_out = pltpu.make_async_copy(whl_s, whl_ref, lsem.at[4])
    whl_out.start()

    for c in first:
        c[0].wait()
    second = []
    for i, d in enumerate((1, 3, 2)):
        second.append(push(GA.at[zz], GA.at[zz], bsend.at[i], brecv.at[i], at_z(d)))
        second[-1].start()
    for c in first:
        c[1].wait()
    for i, d in enumerate((1, 3, 2)):
        second.append(push(GB.at[xx], GB.at[xx], bsend.at[3 + i], brecv.at[3 + i], at_x(d)))
        second[-1].start()

    gram = lax.dot_general(
        whl_s[...], whl_s[...], (((1,), (1,)), ((), ())), preferred_element_type=jnp.float32
    )
    gram = gram[0:128, 0:128] + gram[0:128, 128:256] + gram[128:256, 0:128] + gram[128:256, 128:256]
    for i in range(3):
        part = gram.astype(jnp.bfloat16)
        g_ref[128 * i : 128 * (i + 1)] = part
        gram = gram - part.astype(jnp.float32)

    for c in second:
        c.wait()

    def pick(w, s, core_of):
        sa, na, _, db, nb, _ = acc[w]
        f = jnp.where(s < na, sa + s, db + s)
        used = s < na + nb
        f = jnp.where(used, f, 0)
        j = f // 6
        i = f - j * 6
        ch = j // 2
        z, x = ch // 4, lax.rem(ch, 4)
        here = used & (lax.rem(j, 2) == core_of)
        va = GA[z, x, jnp.minimum(i, 2)]
        vb = GB[x, z, jnp.maximum(i - 3, 0)]
        return jnp.where(here, jnp.where(i < 3, va, vb), jnp.zeros_like(va))

    for s in range(9):
        SEL[s] = pick(1, s, core)
    swap = push(SEL, PART, csend, crecv, partner)
    swap.start()
    mine = [pick(0, s, core) for s in range(9)]
    swap.wait()
    for s in range(9):
        T4[s, strip] = mine[s] + PART[s]
    last = []
    for i, d in enumerate((1, 3, 2)):
        c = pltpu.make_async_remote_copy(
            src_ref=T4.at[:, strip], dst_ref=T4.at[:, strip],
            send_sem=tsend.at[i], recv_sem=trecv.at[i],
            device_id=(lax.rem(strip + d, 4), seq), device_id_type=MESH,
        )
        c.start()
        last.append(c)
    whl_out.wait()
    for c in last:
        c.wait()
    tok_ref[...] = T4[...]


def front(features, conv_weight, latent_weight, embed_weight, frames, owner, offset):
    smem = pl.BlockSpec(memory_space=pltpu.SMEM)
    anys = pl.BlockSpec(memory_space=pl.ANY)
    vmem = pl.BlockSpec(memory_space=pltpu.VMEM)
    bf, f32 = jnp.bfloat16, jnp.float32
    dma = pltpu.SemaphoreType.DMA
    return pl.pallas_call(
        front_kernel,
        in_specs=[smem, smem, smem, anys, anys, anys, anys],
        out_specs=[smem, vmem, anys, vmem],
        out_shape=[
            jax.ShapeDtypeStruct((27,), jnp.int32),
            jax.ShapeDtypeStruct((9, 4, 32, 128), bf),
            jax.ShapeDtypeStruct((256, D), bf),
            jax.ShapeDtypeStruct((384, 128), bf),
        ],
        scratch_shapes=[
            pltpu.VMEM((8, 10, 16, 128), bf),
            pltpu.VMEM((8, 10, 16, 384), bf),
            pltpu.VMEM((3, 1152, 128), bf),
            pltpu.VMEM((512, 128), bf),
            pltpu.VMEM((128, D), bf),
            pltpu.VMEM((8, 128, 384), f32),
            pltpu.VMEM((6, 128, 128), f32),
            pltpu.VMEM((4, 4, 3, 32, 128), bf),
            pltpu.VMEM((4, 4, 3, 32, 128), bf),
            pltpu.VMEM((9, 32, 128), bf),
            pltpu.VMEM((9, 32, 128), bf),
            pltpu.VMEM((9, 4, 32, 128), bf),
            pltpu.VMEM((256, D), bf),
            pltpu.SMEM((8,), jnp.int32),
            dma((5,)), dma((5,)), dma((5,)), dma((6,)), dma((6,)), dma((6,)), dma((6,)),
            dma, dma, dma((3,)), dma((3,)),
        ],
        compiler_params=pltpu.CompilerParams(
            collective_id=0, has_side_effects=True, vmem_limit_bytes=40 * 2**20
        ),
        cost_estimate=pl.CostEstimate(flops=10**9, bytes_accessed=4 * 10**6, transcendentals=10**5),
        name="front",
    )(frames, owner, offset, features, conv_weight.reshape(3, 1152, 128), latent_weight, embed_weight)


def shards(
    features,
    conv_weight,
    latent_weight,
    embed_weight,
    qkv_weight,
    modulation,
    clip_frames,
    clip_owner,
    clip_offset,
):
    seg, tokens, whl, gram = front(
        features, conv_weight, latent_weight, embed_weight, clip_frames, clip_owner, clip_offset
    )
    out = call(seg, tokens.reshape(CAP * PF, 128), whl, gram, modulation, qkv_weight.transpose(1, 0, 2))
    return out.reshape(1, CAP * PF, -1)


def solution(mesh):
    placed = (
        P("seq", "strip", None, None),
        P(),
        P(),
        P(),
        P(None, None, "strip"),
        P(),
        P(),
        P(),
        P(),
    )
    return jax.shard_map(
        shards, mesh=mesh, in_specs=placed, out_specs=P("seq", None, "strip"), check_vma=False
    )
```

```python
import jax
import jax.numpy as jnp
from jax import lax
from jax.experimental import pallas as pl
from jax.experimental.pallas import tpu as pltpu
from jax.sharding import PartitionSpec as P

EPS = 1e-6
HEAD = 128
CAP = 9
PF = 128
D = 3072
NB = 512
C2 = 128**-0.5 * 1.4426950408889634
CUTS = {1: (1,), 2: (2,), 3: (3,), 4: (4,), 5: (5,), 6: (3, 3), 7: (4, 3), 8: (4, 4)}
WIDE = {1: 6, 2: 6, 3: 3, 4: 3, 5: 2, 6: 2, 7: 3, 8: 6}


def attend(q, k, v1):
    s = lax.dot_general(q, k, (((1,), (1,)), ((), ())), preferred_element_type=jnp.float32)
    top = jnp.max(s, axis=1, keepdims=True)
    raised = jnp.exp2((s - top) * C2).astype(jnp.bfloat16)
    o = jnp.dot(raised, v1, preferred_element_type=jnp.float32)
    return (o[:, :HEAD] * (1.0 / o[:, HEAD:])).astype(jnp.bfloat16)


def block_kernel(
    seg_ref, tok_ref, g_ref, whl_ref, mod_ref, w_ref, o_ref,
    mod_s, q_s, k_s, v_s, o_s, osem
):
    T = CAP * PF
    clips = [jnp.maximum(seg_ref[s], 0) for s in range(CAP)]
    valid = [(seg_ref[s] >= 0).astype(jnp.float32) for s in range(CAP)]
    v_s[:, :, HEAD:] = jnp.ones_like(v_s[:, :, HEAD:])

    t = tok_ref[...]
    tt = jnp.concatenate([t, t], axis=1)
    tg = jnp.dot(jnp.concatenate([tt, t], axis=1), g_ref[...], preferred_element_type=jnp.float32)
    var = jnp.sum(tg * t.astype(jnp.float32), axis=1, keepdims=True) * (1.0 / D)
    rstd = lax.rsqrt(jnp.maximum(var, 0.0) + EPS)

    def norm(n, _):
        cols = pl.ds(pl.multiple_of(n * NB, NB), NB)
        x = jnp.dot(tt, whl_ref[:, cols], preferred_element_type=jnp.float32)
        for s in range(CAP):
            shift = mod_ref[clips[s], 0:1, cols].astype(jnp.float32) * valid[s]
            scale = 1.0 + mod_ref[clips[s], 1:2, cols].astype(jnp.float32) * valid[s]
            rows = slice(s * PF, (s + 1) * PF)
            mod_s[rows, cols] = ((x[rows] * rstd[rows]) * scale + shift).astype(jnp.bfloat16)
        return 0

    lax.fori_loop(0, D // NB, norm, 0)

    def split(y, ref, h0):
        for i in range(y.shape[1] // HEAD):
            ref[h0 + i, :, 0:HEAD] = y[:, i * HEAD : (i + 1) * HEAD]

    for i in range(5):
        if i < 3:
            w = w_ref[i, :, 0:512]
        elif i == 3:
            w = jnp.concatenate([w_ref[0, :, 512:768], w_ref[1, :, 512:768]], axis=1)
        else:
            w = w_ref[2, :, 512:768]
        y = jnp.dot(mod_s[...], w, preferred_element_type=jnp.float32).astype(jnp.bfloat16)
        if i < 3:
            split(y, (q_s, k_s, v_s)[i], 0)
        elif i == 3:
            split(y[:, 0:256], q_s, 4)
            split(y[:, 256:512], k_s, 4)
        else:
            split(y, v_s, 4)

    def write(h):
        cols = pl.ds(pl.multiple_of(h * HEAD, HEAD), HEAD)
        return pltpu.make_async_copy(o_s.at[h], o_ref.at[:, cols], osem.at[h])

    def segment(a):
        n = seg_ref[2 * CAP + a]
        base = pl.multiple_of(a * PF, PF)
        for nn in CUTS:
            @pl.when(n == nn)
            def _():
                keys = pl.ds(base, nn * PF)
                def heads(hh, _):
                    for u in range(WIDE[nn]):
                        h = hh * WIDE[nn] + u
                        i = 0
                        for c in CUTS[nn]:
                            rows = pl.ds(pl.multiple_of(base + i * PF, PF), c * PF)
                            o_s[h, rows] = attend(q_s[h, rows], k_s[h, keys], v_s[h, keys])
                            i += c
                    return 0

                lax.fori_loop(0, 6 // WIDE[nn], heads, 0)

        return a + n

    lax.while_loop(lambda a: a < CAP, segment, jnp.int32(0))
    for h in range(6):
        write(h).start()
    for h in range(6):
        write(h).wait()


def call(seg, tokens, whl, ghl, mod, w3):
    T = CAP * PF
    bf = jnp.bfloat16
    hbm = pl.BlockSpec(memory_space=pltpu.HBM)
    vmem = pl.BlockSpec(memory_space=pltpu.VMEM)
    dma = pltpu.SemaphoreType.DMA
    return pl.pallas_call(
        block_kernel,
        in_specs=[pl.BlockSpec(memory_space=pltpu.SMEM), vmem, vmem, vmem, vmem, vmem],
        out_specs=hbm,
        out_shape=jax.ShapeDtypeStruct((T, 768), bf),
        scratch_shapes=[
            pltpu.VMEM((T, D), bf),
            pltpu.VMEM((6, T, HEAD), bf), pltpu.VMEM((6, T, HEAD), bf), pltpu.VMEM((6, T, 256), bf),
            pltpu.VMEM((6, T, HEAD), bf),
            dma((6,)),
        ],
        compiler_params=pltpu.CompilerParams(vmem_limit_bytes=36 * 2**20),
        cost_estimate=pl.CostEstimate(flops=2 * 10**10, bytes_accessed=2 * 10**7, transcendentals=8 * 10**6),
        name="block",
    )(seg, tokens, ghl, whl, mod, pltpu.with_memory_space_constraint(w3, pltpu.VMEM))


MESH = pl.DeviceIdType.MESH


def front_kernel(
    frames_ref, owner_ref, offset_ref, feat_ref, conv_ref, lat_ref, embed_ref,
    seg_ref, tok_ref, whl_ref, g_ref,
    F, X3, Wv, Lv, Ev, P, A, GA, GB, SEL, PART, T4, whl_s, kflag,
    lsem, hsend, hrecv, asend, arecv, bsend, brecv, csend, crecv, tsend, trecv,
):
    strip = lax.axis_index("strip")
    seq = lax.axis_index("seq")
    core = lax.rem(seq, 2)
    chip = seq // 2
    xx = lax.rem(chip, 4)
    zz = chip // 4
    up, down = lax.rem(strip + 3, 4), lax.rem(strip + 1, 4)
    prev, nxt = lax.rem(seq + 31, 32), lax.rem(seq + 1, 32)

    def at_x(d):
        return (zz * 4 + lax.rem(xx + d, 4)) * 2 + core

    def at_z(d):
        return (lax.rem(zz + d, 4) * 4 + xx) * 2 + core

    partner = chip * 2 + 1 - core

    loc = [
        pltpu.make_async_copy(feat_ref, F.at[2:8, 1:9], lsem.at[0]),
        pltpu.make_async_copy(conv_ref, Wv, lsem.at[1]),
        pltpu.make_async_copy(lat_ref, Lv, lsem.at[2]),
        pltpu.make_async_copy(embed_ref, Ev, lsem.at[3]),
    ]
    for c in loc:
        c.start()

    barrier = pltpu.get_barrier_semaphore()

    def hello(s, j):
        pl.semaphore_signal(barrier, inc=1, device_id=(s, j), device_id_type=MESH)

    for d in (1, 2, 3):
        hello(strip, at_x(d))
        hello(strip, at_z(d))
        hello(lax.rem(strip + d, 4), seq)
    hello(strip, partner)
    hello(up, prev)
    hello(down, prev)

    @pl.when(core == 0)
    def _():
        hello(strip, prev)

    base = seq * 6
    own = (seq, partner)
    zero = jnp.int32(0)

    def clip(c, carry):
        start, flags, acc = carry
        n, o, off = frames_ref[c], owner_ref[c], offset_ref[c]
        flags = tuple(jnp.where(start == base - 1 + i, 1, flags[i]) for i in range(7))
        out = []
        for w in range(2):
            sa, na, ca, db, nb, cb = acc[w]
            is_a = (o == own[w]) & (off == 0)
            is_b = (o == own[w]) & (off > 0)
            out.append((
                jnp.where(is_a, start, sa), jnp.where(is_a, n, na), jnp.where(is_a, c, ca),
                jnp.where(is_b, start - off, db), jnp.where(is_b, n, nb), jnp.where(is_b, c, cb),
            ))
        return start + n, flags, tuple(out)

    _, flags, acc = lax.fori_loop(
        0, 64, clip, (zero, (zero,) * 7, ((zero,) * 6,) * 2), unroll=4
    )
    sa, na, ca, db, nb, cb = acc[0]
    for s in range(9):
        in_a = s < na
        in_b = (s >= na) & (s < na + nb)
        seg_ref[s] = jnp.where(in_a, ca, jnp.where(in_b, cb, -1))
        seg_ref[9 + s] = jnp.where(in_a, 0, jnp.where(in_b, na, na + nb))
        seg_ref[18 + s] = jnp.where(in_a, na, jnp.where(in_b, nb, 9 - na - nb))

    loc[0].wait()
    pl.semaphore_wait(barrier, 12 + core)

    halo = []

    def send(src, dst, s, j):
        i = len(halo)
        c = pltpu.make_async_remote_copy(
            src_ref=src, dst_ref=dst, send_sem=hsend.at[i], recv_sem=hrecv.at[i],
            device_id=(s, j), device_id_type=MESH,
        )
        c.start()
        halo.append(c)

    send(F.at[6:8, 1:9], F.at[0:2, 1:9], strip, nxt)
    send(F.at[2:8, 8], F.at[2:8, 0], down, seq)
    send(F.at[2:8, 1], F.at[2:8, 9], up, seq)
    send(F.at[6:8, 8], F.at[0:2, 0], down, nxt)
    send(F.at[6:8, 1], F.at[0:2, 9], up, nxt)
    for c in halo:
        c.wait()

    @pl.when(strip == 0)
    def _():
        F[:, 0] = jnp.zeros_like(F[:, 0])

    @pl.when(strip == 3)
    def _():
        F[:, 9] = jnp.zeros_like(F[:, 9])

    def widen(g, _):
        x = F[g].reshape(160, 128).astype(jnp.float32)
        col = lax.rem(lax.broadcasted_iota(jnp.int32, (160, 128), 0), 16)
        left = jnp.where(col == 0, 0.0, pltpu.roll(x, 1, 0))
        right = jnp.where(col == 15, 0.0, pltpu.roll(x, 159, 0))
        X3[g, :, :, 0:128] = left.astype(jnp.bfloat16).reshape(10, 16, 128)
        X3[g, :, :, 128:256] = F[g]
        X3[g, :, :, 256:384] = right.astype(jnp.bfloat16).reshape(10, 16, 128)
        return 0

    lax.fori_loop(0, 8, widen, 0)
    loc[1].wait()
    rhs = jnp.concatenate([Wv[0], Wv[1], Wv[2]], axis=1)

    def taps(g, _):
        lhs = jnp.concatenate(
            [X3[g, d : d + 8].reshape(128, 384) for d in range(3)], axis=1
        )
        P[g] = jnp.dot(lhs, rhs, preferred_element_type=jnp.float32)
        return 0

    lax.fori_loop(0, 8, taps, 0)
    for f in range(6):
        not_start = 1 - flags[f + 1]
        k1 = not_start.astype(jnp.float32)
        k2 = (not_start * (1 - flags[f])).astype(jnp.float32)
        h = P[f + 2, :, 0:128] + k1 * P[f + 1, :, 128:256] + k2 * P[f, :, 256:384]
        a = h / (1.0 + jnp.exp(-h))
        A[f] = a.astype(jnp.bfloat16).astype(jnp.float32)
    loc[2].wait()
    for f in range(6):
        even = A[f, pl.ds(0, 64, stride=2)].reshape(4, 2, 8, 128)
        odd = A[f, pl.ds(1, 64, stride=2)].reshape(4, 2, 8, 128)
        patch = jnp.concatenate(
            [v[:, a].reshape(32, 128) for a in range(2) for v in (even, odd)], axis=1
        ).astype(jnp.bfloat16)
        lat = jnp.dot(patch, Lv[...], preferred_element_type=jnp.float32).astype(jnp.bfloat16)
        if f < 3:
            GA[zz, xx, f] = lat
        else:
            GB[xx, zz, f - 3] = lat

    def push(src, dst, ss, rs, j):
        return pltpu.make_async_remote_copy(
            src_ref=src, dst_ref=dst, send_sem=ss, recv_sem=rs,
            device_id=(strip, j), device_id_type=MESH,
        )

    first = []
    for i, d in enumerate((1, 3, 2)):
        first.append((
            push(GA.at[zz, xx], GA.at[zz, xx], asend.at[i], arecv.at[i], at_x(d)),
            push(GB.at[xx, zz], GB.at[xx, zz], asend.at[3 + i], arecv.at[3 + i], at_z(d)),
        ))
        for c in first[-1]:
            c.start()

    loc[3].wait()
    w = Ev[...].astype(jnp.float32)
    wc = w - jnp.mean(w, axis=1, keepdims=True)
    hi = wc.astype(jnp.bfloat16)
    lo = (wc - hi.astype(jnp.float32)).astype(jnp.bfloat16)
    whl_s[0:128] = hi
    whl_s[128:256] = lo
    whl_out = pltpu.make_async_copy(whl_s, whl_ref, lsem.at[4])
    whl_out.start()

    for c in first:
        c[0].wait()
    second = []
    for i, d in enumerate((1, 3, 2)):
        second.append(push(GA.at[zz], GA.at[zz], bsend.at[i], brecv.at[i], at_z(d)))
        second[-1].start()
    for c in first:
        c[1].wait()
    for i, d in enumerate((1, 3, 2)):
        second.append(push(GB.at[xx], GB.at[xx], bsend.at[3 + i], brecv.at[3 + i], at_x(d)))
        second[-1].start()

    gram = lax.dot_general(
        whl_s[...], whl_s[...], (((1,), (1,)), ((), ())), preferred_element_type=jnp.float32
    )
    gram = gram[0:128, 0:128] + gram[0:128, 128:256] + gram[128:256, 0:128] + gram[128:256, 128:256]
    for i in range(3):
        part = gram.astype(jnp.bfloat16)
        g_ref[128 * i : 128 * (i + 1)] = part
        gram = gram - part.astype(jnp.float32)

    for c in second:
        c.wait()

    def pick(w, s, core_of):
        sa, na, _, db, nb, _ = acc[w]
        f = jnp.where(s < na, sa + s, db + s)
        used = s < na + nb
        f = jnp.where(used, f, 0)
        j = f // 6
        i = f - j * 6
        ch = j // 2
        z, x = ch // 4, lax.rem(ch, 4)
        here = used & (lax.rem(j, 2) == core_of)
        va = GA[z, x, jnp.minimum(i, 2)]
        vb = GB[x, z, jnp.maximum(i - 3, 0)]
        return jnp.where(here, jnp.where(i < 3, va, vb), jnp.zeros_like(va))

    for s in range(9):
        SEL[s] = pick(1, s, core)
    swap = push(SEL, PART, csend, crecv, partner)
    swap.start()
    mine = [pick(0, s, core) for s in range(9)]
    swap.wait()
    for s in range(9):
        T4[s, strip] = mine[s] + PART[s]
    last = []
    for i, d in enumerate((1, 3, 2)):
        c = pltpu.make_async_remote_copy(
            src_ref=T4.at[:, strip], dst_ref=T4.at[:, strip],
            send_sem=tsend.at[i], recv_sem=trecv.at[i],
            device_id=(lax.rem(strip + d, 4), seq), device_id_type=MESH,
        )
        c.start()
        last.append(c)
    whl_out.wait()
    for c in last:
        c.wait()
    tok_ref[...] = T4[...]


def front(features, conv_weight, latent_weight, embed_weight, frames, owner, offset):
    smem = pl.BlockSpec(memory_space=pltpu.SMEM)
    anys = pl.BlockSpec(memory_space=pltpu.HBM)
    vmem = pl.BlockSpec(memory_space=pltpu.VMEM)
    bf, f32 = jnp.bfloat16, jnp.float32
    dma = pltpu.SemaphoreType.DMA
    return pl.pallas_call(
        front_kernel,
        in_specs=[smem, smem, smem, anys, anys, anys, anys],
        out_specs=[smem, vmem, anys, vmem],
        out_shape=[
            jax.ShapeDtypeStruct((27,), jnp.int32),
            jax.ShapeDtypeStruct((9, 4, 32, 128), bf),
            jax.ShapeDtypeStruct((256, D), bf),
            jax.ShapeDtypeStruct((384, 128), bf),
        ],
        scratch_shapes=[
            pltpu.VMEM((8, 10, 16, 128), bf),
            pltpu.VMEM((8, 10, 16, 384), bf),
            pltpu.VMEM((3, 1152, 128), bf),
            pltpu.VMEM((512, 128), bf),
            pltpu.VMEM((128, D), bf),
            pltpu.VMEM((8, 128, 384), f32),
            pltpu.VMEM((6, 128, 128), f32),
            pltpu.VMEM((4, 4, 3, 32, 128), bf),
            pltpu.VMEM((4, 4, 3, 32, 128), bf),
            pltpu.VMEM((9, 32, 128), bf),
            pltpu.VMEM((9, 32, 128), bf),
            pltpu.VMEM((9, 4, 32, 128), bf),
            pltpu.VMEM((256, D), bf),
            pltpu.SMEM((8,), jnp.int32),
            dma((5,)), dma((5,)), dma((5,)), dma((6,)), dma((6,)), dma((6,)), dma((6,)),
            dma, dma, dma((3,)), dma((3,)),
        ],
        compiler_params=pltpu.CompilerParams(
            collective_id=0, has_side_effects=True, vmem_limit_bytes=12 * 2**20
        ),
        cost_estimate=pl.CostEstimate(flops=2 * 10**10, bytes_accessed=6 * 10**7, transcendentals=10**5),
        name="front",
    )(*(pltpu.with_memory_space_constraint(x, pltpu.HBM) for x in (frames, owner, offset, features, conv_weight.reshape(3, 1152, 128), latent_weight, embed_weight)))


def shards(
    features,
    conv_weight,
    latent_weight,
    embed_weight,
    qkv_weight,
    modulation,
    clip_frames,
    clip_owner,
    clip_offset,
):
    seg, tokens, whl, gram = front(
        features, conv_weight, latent_weight, embed_weight, clip_frames, clip_owner, clip_offset
    )
    out = call(seg, tokens.reshape(CAP * PF, 128), whl, gram, modulation, qkv_weight.transpose(1, 0, 2))
    return out.reshape(1, CAP * PF, -1)


def solution(mesh):
    placed = (
        P("seq", "strip", None, None),
        P(),
        P(),
        P(),
        P(None, None, "strip"),
        P(),
        P(),
        P(),
        P(),
    )
    return jax.shard_map(
        shards, mesh=mesh, in_specs=placed, out_specs=P("seq", None, "strip"), check_vma=False
    )
```

```python
import jax
import jax.numpy as jnp
from jax import lax
from jax.experimental import pallas as pl
from jax.experimental.pallas import tpu as pltpu
from jax.sharding import PartitionSpec as P

EPS = 1e-6
HEAD = 128
CAP = 9
PF = 128
D = 3072
NB = 512
C2 = 128**-0.5 * 1.4426950408889634
CUTS = {1: (1,), 2: (2,), 3: (3,), 4: (4,), 5: (5,), 6: (3, 3), 7: (4, 3), 8: (4, 4)}
WIDE = {1: 6, 2: 6, 3: 3, 4: 3, 5: 2, 6: 2, 7: 3, 8: 6}


def attend(q, k, v1):
    s = lax.dot_general(q, k, (((1,), (1,)), ((), ())), preferred_element_type=jnp.float32)
    top = jnp.max(s, axis=1, keepdims=True)
    raised = jnp.exp2((s - top) * C2).astype(jnp.bfloat16)
    o = jnp.dot(raised, v1, preferred_element_type=jnp.float32)
    return (o[:, :HEAD] * (1.0 / o[:, HEAD:])).astype(jnp.bfloat16)


def block_kernel(
    seg_ref, tok_ref, g_ref, whl_ref, mod_ref, w_ref, o_ref,
    mod_s, q_s, k_s, v_s, o_s, osem
):
    T = CAP * PF
    clips = [jnp.maximum(seg_ref[s], 0) for s in range(CAP)]
    valid = [(seg_ref[s] >= 0).astype(jnp.float32) for s in range(CAP)]
    v_s[:, :, HEAD:] = jnp.ones_like(v_s[:, :, HEAD:])

    t = tok_ref[...]
    tt = jnp.concatenate([t, t], axis=1)
    tg = jnp.dot(jnp.concatenate([tt, t], axis=1), g_ref[...], preferred_element_type=jnp.float32)
    var = jnp.sum(tg * t.astype(jnp.float32), axis=1, keepdims=True) * (1.0 / D)
    rstd = lax.rsqrt(jnp.maximum(var, 0.0) + EPS)

    def norm(n, _):
        cols = pl.ds(pl.multiple_of(n * NB, NB), NB)
        x = jnp.dot(tt, whl_ref[:, cols], preferred_element_type=jnp.float32)
        for s in range(CAP):
            shift = mod_ref[clips[s], 0:1, cols].astype(jnp.float32) * valid[s]
            scale = 1.0 + mod_ref[clips[s], 1:2, cols].astype(jnp.float32) * valid[s]
            rows = slice(s * PF, (s + 1) * PF)
            mod_s[rows, cols] = ((x[rows] * rstd[rows]) * scale + shift).astype(jnp.bfloat16)
        return 0

    lax.fori_loop(0, D // NB, norm, 0)

    def split(y, ref, h0):
        for i in range(y.shape[1] // HEAD):
            ref[h0 + i, :, 0:HEAD] = y[:, i * HEAD : (i + 1) * HEAD]

    for i in range(5):
        if i < 3:
            w = w_ref[i, :, 0:512]
        elif i == 3:
            w = jnp.concatenate([w_ref[0, :, 512:768], w_ref[1, :, 512:768]], axis=1)
        else:
            w = w_ref[2, :, 512:768]
        y = jnp.dot(mod_s[...], w, preferred_element_type=jnp.float32).astype(jnp.bfloat16)
        if i < 3:
            split(y, (q_s, k_s, v_s)[i], 0)
        elif i == 3:
            split(y[:, 0:256], q_s, 4)
            split(y[:, 256:512], k_s, 4)
        else:
            split(y, v_s, 4)

    def write(h):
        cols = pl.ds(pl.multiple_of(h * HEAD, HEAD), HEAD)
        return pltpu.make_async_copy(o_s.at[h], o_ref.at[:, cols], osem.at[h])

    def segment(a):
        n = seg_ref[2 * CAP + a]
        base = pl.multiple_of(a * PF, PF)
        for nn in CUTS:
            @pl.when(n == nn)
            def _():
                keys = pl.ds(base, nn * PF)
                def heads(hh, _):
                    for u in range(WIDE[nn]):
                        h = hh * WIDE[nn] + u
                        i = 0
                        for c in CUTS[nn]:
                            rows = pl.ds(pl.multiple_of(base + i * PF, PF), c * PF)
                            o_s[h, rows] = attend(q_s[h, rows], k_s[h, keys], v_s[h, keys])
                            i += c
                    return 0

                lax.fori_loop(0, 6 // WIDE[nn], heads, 0)

        return a + n

    lax.while_loop(lambda a: a < CAP, segment, jnp.int32(0))
    for h in range(6):
        write(h).start()
    for h in range(6):
        write(h).wait()


def call(seg, tokens, whl, ghl, mod, w3):
    T = CAP * PF
    bf = jnp.bfloat16
    hbm = pl.BlockSpec(memory_space=pltpu.HBM)
    vmem = pl.BlockSpec(memory_space=pltpu.VMEM)
    dma = pltpu.SemaphoreType.DMA
    return pl.pallas_call(
        block_kernel,
        in_specs=[pl.BlockSpec(memory_space=pltpu.SMEM), vmem, vmem, vmem, vmem, vmem],
        out_specs=hbm,
        out_shape=jax.ShapeDtypeStruct((T, 768), bf),
        scratch_shapes=[
            pltpu.VMEM((T, D), bf),
            pltpu.VMEM((6, T, HEAD), bf), pltpu.VMEM((6, T, HEAD), bf), pltpu.VMEM((6, T, 256), bf),
            pltpu.VMEM((6, T, HEAD), bf),
            dma((6,)),
        ],
        compiler_params=pltpu.CompilerParams(vmem_limit_bytes=36 * 2**20),
        cost_estimate=pl.CostEstimate(flops=2 * 10**10, bytes_accessed=2 * 10**7, transcendentals=8 * 10**6),
        name="block",
    )(seg, tokens, ghl, whl, mod, pltpu.with_memory_space_constraint(w3, pltpu.VMEM))


MESH = pl.DeviceIdType.MESH


def front_kernel(
    frames_ref, owner_ref, offset_ref, feat_ref, conv_ref, lat_ref, embed_ref,
    seg_ref, tok_ref, whl_ref, g_ref,
    F, X3, Wv, Lv, Ev, P, A, GA, GB, SEL, PART, T4,
    lsem, hsend, hrecv, asend, arecv, bsend, brecv, csend, crecv, tsend, trecv,
):
    strip = lax.axis_index("strip")
    seq = lax.axis_index("seq")
    core = lax.rem(seq, 2)
    chip = seq // 2
    xx = lax.rem(chip, 4)
    zz = chip // 4
    up, down = lax.rem(strip + 3, 4), lax.rem(strip + 1, 4)
    prev, nxt = lax.rem(seq + 31, 32), lax.rem(seq + 1, 32)

    def at_x(d):
        return (zz * 4 + lax.rem(xx + d, 4)) * 2 + core

    def at_z(d):
        return (lax.rem(zz + d, 4) * 4 + xx) * 2 + core

    partner = chip * 2 + 1 - core

    loc = [
        pltpu.make_async_copy(feat_ref, F.at[2:8, 1:9], lsem.at[0]),
        pltpu.make_async_copy(conv_ref, Wv, lsem.at[1]),
        pltpu.make_async_copy(lat_ref, Lv, lsem.at[2]),
        pltpu.make_async_copy(embed_ref, Ev, lsem.at[3]),
    ]
    for c in loc:
        c.start()

    barrier = pltpu.get_barrier_semaphore()

    def hello(s, j):
        pl.semaphore_signal(barrier, inc=1, device_id=(s, j), device_id_type=MESH)

    for d in (1, 2, 3):
        hello(strip, at_x(d))
        hello(strip, at_z(d))
        hello(lax.rem(strip + d, 4), seq)
    hello(strip, partner)
    hello(up, prev)
    hello(down, prev)

    @pl.when(core == 0)
    def _():
        hello(strip, prev)

    loc[0].wait()
    pl.semaphore_wait(barrier, 12 + core)

    halo = []

    def send(src, dst, s, j):
        i = len(halo)
        c = pltpu.make_async_remote_copy(
            src_ref=src, dst_ref=dst, send_sem=hsend.at[i], recv_sem=hrecv.at[i],
            device_id=(s, j), device_id_type=MESH,
        )
        c.start()
        halo.append(c)

    send(F.at[6:8, 1:9], F.at[0:2, 1:9], strip, nxt)
    send(F.at[2:8, 8], F.at[2:8, 0], down, seq)
    send(F.at[2:8, 1], F.at[2:8, 9], up, seq)
    send(F.at[6:8, 8], F.at[0:2, 0], down, nxt)
    send(F.at[6:8, 1], F.at[0:2, 9], up, nxt)
    base = seq * 6
    own = (seq, partner)
    zero = jnp.int32(0)

    def clip(c, carry):
        start, flags, acc = carry
        n, o, off = frames_ref[c], owner_ref[c], offset_ref[c]
        flags = tuple(jnp.where(start == base - 1 + i, 1, flags[i]) for i in range(7))
        out = []
        for w in range(2):
            sa, na, ca, db, nb, cb = acc[w]
            is_a = (o == own[w]) & (off == 0)
            is_b = (o == own[w]) & (off > 0)
            out.append((
                jnp.where(is_a, start, sa), jnp.where(is_a, n, na), jnp.where(is_a, c, ca),
                jnp.where(is_b, start - off, db), jnp.where(is_b, n, nb), jnp.where(is_b, c, cb),
            ))
        return start + n, flags, tuple(out)

    _, flags, acc = lax.fori_loop(
        0, 64, clip, (zero, (zero,) * 7, ((zero,) * 6,) * 2), unroll=4
    )
    sa, na, ca, db, nb, cb = acc[0]
    for s in range(9):
        in_a = s < na
        in_b = (s >= na) & (s < na + nb)
        seg_ref[s] = jnp.where(in_a, ca, jnp.where(in_b, cb, -1))
        seg_ref[9 + s] = jnp.where(in_a, 0, jnp.where(in_b, na, na + nb))
        seg_ref[18 + s] = jnp.where(in_a, na, jnp.where(in_b, nb, 9 - na - nb))

    def widen(g, lo, hi):
        n = (hi - lo) * 16
        x = F[g, lo:hi].reshape(n, 128).astype(jnp.float32)
        col = lax.rem(lax.broadcasted_iota(jnp.int32, (n, 128), 0), 16)
        left = jnp.where(col == 0, 0.0, pltpu.roll(x, 1, 0))
        right = jnp.where(col == 15, 0.0, pltpu.roll(x, n - 1, 0))
        X3[g, lo:hi, :, 0:128] = left.astype(jnp.bfloat16).reshape(hi - lo, 16, 128)
        X3[g, lo:hi, :, 128:256] = F[g, lo:hi]
        X3[g, lo:hi, :, 256:384] = right.astype(jnp.bfloat16).reshape(hi - lo, 16, 128)

    def edges(lo, hi):
        @pl.when(strip == 0)
        def _():
            F[lo:hi, 0] = jnp.zeros_like(F[lo:hi, 0])

        @pl.when(strip == 3)
        def _():
            F[lo:hi, 9] = jnp.zeros_like(F[lo:hi, 9])

    def window(g, d):
        return X3[g, d : d + 8].reshape(128, 384)

    def weight(d):
        return jnp.concatenate([Wv[t, 384 * d : 384 * (d + 1)] for t in range(3)], axis=1)

    def middle(g, _):
        widen(g, 1, 9)
        P[g] = jnp.dot(window(g, 1), weight(1), preferred_element_type=jnp.float32)
        return 0

    def outer(g, _):
        widen(g, 0, 1)
        widen(g, 9, 10)
        P[g] += jnp.dot(
            jnp.concatenate([window(g, 0), window(g, 2)], axis=1),
            jnp.concatenate([weight(0), weight(2)], axis=0),
            preferred_element_type=jnp.float32,
        )
        return 0

    def token(f):
        not_start = 1 - flags[f + 1]
        k1 = not_start.astype(jnp.float32)
        k2 = (not_start * (1 - flags[f])).astype(jnp.float32)
        h = P[f + 2, :, 0:128] + k1 * P[f + 1, :, 128:256] + k2 * P[f, :, 256:384]
        a = h / (1.0 + jnp.exp(-h))
        A[f] = a.astype(jnp.bfloat16).astype(jnp.float32)
        even = A[f, pl.ds(0, 64, stride=2)].reshape(4, 2, 8, 128)
        odd = A[f, pl.ds(1, 64, stride=2)].reshape(4, 2, 8, 128)
        patch = jnp.concatenate(
            [v[:, a].reshape(32, 128) for a in range(2) for v in (even, odd)], axis=1
        ).astype(jnp.bfloat16)
        return jnp.dot(patch, Lv[...], preferred_element_type=jnp.float32).astype(jnp.bfloat16)

    def push(src, ss, rs, j):
        c = pltpu.make_async_remote_copy(
            src_ref=src, dst_ref=src, send_sem=ss, recv_sem=rs,
            device_id=(strip, j), device_id_type=MESH,
        )
        c.start()
        return c

    loc[1].wait()
    lax.fori_loop(2, 8, middle, 0)
    loc[2].wait()
    for c in halo[1:3]:
        c.wait()
    edges(2, 8)
    lax.fori_loop(2, 8, outer, 0)
    for f in range(2, 6):
        GB[xx, zz, f - 2] = token(f)
    near_b = [
        push(GB.at[xx, zz], asend.at[3 + i], arecv.at[3 + i], at_z(d))
        for i, d in enumerate((2, 1, 3))
    ]
    halo[0].wait()
    for c in halo[3:]:
        c.wait()
    edges(0, 2)
    lax.fori_loop(0, 2, middle, 0)
    lax.fori_loop(0, 2, outer, 0)
    for f in range(2):
        GA[zz, xx, f] = token(f)
    near_a = [
        push(GA.at[zz, xx], asend.at[i], arecv.at[i], at_x(d)) for i, d in enumerate((2, 1, 3))
    ]
    for c in near_b:
        c.wait()
    far = [
        push(GB.at[xx], bsend.at[3 + i], brecv.at[3 + i], at_x(d))
        for i, d in enumerate((2, 1, 3))
    ]
    for c in near_a:
        c.wait()
    far += [
        push(GA.at[zz], bsend.at[i], brecv.at[i], at_z(d)) for i, d in enumerate((2, 1, 3))
    ]

    loc[3].wait()
    w = Ev[...].astype(jnp.float32)
    wc = w - jnp.mean(w, axis=1, keepdims=True)
    hi = wc.astype(jnp.bfloat16)
    whl_ref[0:128] = hi
    whl_ref[128:256] = (wc - hi.astype(jnp.float32)).astype(jnp.bfloat16)
    gram = lax.dot_general(
        whl_ref[...], whl_ref[...], (((1,), (1,)), ((), ())), preferred_element_type=jnp.float32
    )
    gram = gram[0:128, 0:128] + gram[0:128, 128:256] + gram[128:256, 0:128] + gram[128:256, 128:256]
    for i in range(3):
        part = gram.astype(jnp.bfloat16)
        g_ref[128 * i : 128 * (i + 1)] = part
        gram = gram - part.astype(jnp.float32)


    for c in far:
        c.wait()

    def pick(w, s, core_of):
        sa, na, _, db, nb, _ = acc[w]
        f = jnp.where(s < na, sa + s, db + s)
        used = s < na + nb
        f = jnp.where(used, f, 0)
        j = f // 6
        i = f - j * 6
        ch = j // 2
        z, x = ch // 4, lax.rem(ch, 4)
        here = used & (lax.rem(j, 2) == core_of)
        va = GA[z, x, jnp.minimum(i, 1)]
        vb = GB[x, z, jnp.maximum(i - 2, 0)]
        return jnp.where(here, jnp.where(i < 2, va, vb), jnp.zeros_like(va))

    for s in range(9):
        SEL[s] = pick(1, s, core)
    swap = pltpu.make_async_remote_copy(
        src_ref=SEL, dst_ref=PART, send_sem=csend, recv_sem=crecv,
        device_id=(strip, partner), device_id_type=MESH,
    )
    swap.start()
    mine = [pick(0, s, core) for s in range(9)]
    swap.wait()
    for s in range(9):
        T4[s, strip] = mine[s] + PART[s]
    last = []
    for i, d in enumerate((2, 1, 3)):
        c = pltpu.make_async_remote_copy(
            src_ref=T4.at[:, strip], dst_ref=T4.at[:, strip],
            send_sem=tsend.at[i], recv_sem=trecv.at[i],
            device_id=(lax.rem(strip + d, 4), seq), device_id_type=MESH,
        )
        c.start()
        last.append(c)
    for c in last:
        c.wait()
    tok_ref[...] = T4[...]


def front(features, conv_weight, latent_weight, embed_weight, frames, owner, offset):
    smem = pl.BlockSpec(memory_space=pltpu.SMEM)
    anys = pl.BlockSpec(memory_space=pltpu.HBM)
    vmem = pl.BlockSpec(memory_space=pltpu.VMEM)
    bf, f32 = jnp.bfloat16, jnp.float32
    dma = pltpu.SemaphoreType.DMA
    return pl.pallas_call(
        front_kernel,
        in_specs=[smem, smem, smem, anys, anys, anys, anys],
        out_specs=[smem, vmem, vmem, vmem],
        out_shape=[
            jax.ShapeDtypeStruct((27,), jnp.int32),
            jax.ShapeDtypeStruct((9, 4, 32, 128), bf),
            jax.ShapeDtypeStruct((256, D), bf),
            jax.ShapeDtypeStruct((384, 128), bf),
        ],
        scratch_shapes=[
            pltpu.VMEM((8, 10, 16, 128), bf),
            pltpu.VMEM((8, 10, 16, 384), bf),
            pltpu.VMEM((3, 1152, 128), bf),
            pltpu.VMEM((512, 128), bf),
            pltpu.VMEM((128, D), bf),
            pltpu.VMEM((8, 128, 384), f32),
            pltpu.VMEM((6, 128, 128), f32),
            pltpu.VMEM((4, 4, 2, 32, 128), bf),
            pltpu.VMEM((4, 4, 4, 32, 128), bf),
            pltpu.VMEM((9, 32, 128), bf),
            pltpu.VMEM((9, 32, 128), bf),
            pltpu.VMEM((9, 4, 32, 128), bf),
            dma((4,)), dma((5,)), dma((5,)), dma((6,)), dma((6,)), dma((6,)), dma((6,)),
            dma, dma, dma((3,)), dma((3,)),
        ],
        compiler_params=pltpu.CompilerParams(
            collective_id=0, has_side_effects=True, vmem_limit_bytes=12 * 2**20
        ),
        cost_estimate=pl.CostEstimate(flops=2 * 10**10, bytes_accessed=6 * 10**7, transcendentals=10**5),
        name="front",
    )(*(pltpu.with_memory_space_constraint(x, pltpu.HBM) for x in (frames, owner, offset, features, conv_weight.reshape(3, 1152, 128), latent_weight, embed_weight)))


def shards(
    features,
    conv_weight,
    latent_weight,
    embed_weight,
    qkv_weight,
    modulation,
    clip_frames,
    clip_owner,
    clip_offset,
):
    seg, tokens, whl, gram = front(
        features, conv_weight, latent_weight, embed_weight, clip_frames, clip_owner, clip_offset
    )
    out = call(seg, tokens.reshape(CAP * PF, 128), whl, gram, modulation, qkv_weight.transpose(1, 0, 2))
    return out.reshape(1, CAP * PF, -1)


def solution(mesh):
    placed = (
        P("seq", "strip", None, None),
        P(),
        P(),
        P(),
        P(None, None, "strip"),
        P(),
        P(),
        P(),
        P(),
    )
    return jax.shard_map(
        shards, mesh=mesh, in_specs=placed, out_specs=P("seq", None, "strip"), check_vma=False
    )
```
